256 devices in a mesh: front: 32 (over z, x), row: 4 (over y), col: 2 (over core).
Axes of the slice: x: 4, y: 4, z: 8, core: 2. Of those that a mesh axis runs over, the one named last changes fastest.
Arguments:
- panel: float32 [32, 32, 512, 512], P('front', None, 'row', 'col'), may hold values from -6 to 13
- children: float32 [64, 4, 512, 512], P('front', None, 'row', 'col'), may hold values from -3 to 3
- parents: int32 [64], replicated, may hold values from 0 to 31, as said below
- row_maps: int32 [64, 16], replicated, may hold values from 0 to 127, as said below
- orders: int32 [32], P('front'), may hold values from 8192 to 16384, as said below
- pivots: int32 [32], P('front'), may hold values from 1 to 256, as said below
Outputs:
- factored: float32 [32, 32, 512, 512], P('front', None, 'row', 'col')
The draws below stay inside these ranges and needn't reach their ends.
Inputs may be any that keep to these rules, and one draw needn't show every extreme that they name: `parents`: child 2 * d has parent p(d) and child 2 * d + 1 has parent (p(d) + r) mod 32, where p is a permutation of the fronts and r is one number in 1 to 31. The row blocks of one child map to distinct blocks, all below orders[parents[c]] / 128; row_maps[c, i] - i is a multiple of 4. Some child reaches block 127. `orders`: multiples of 128; some front has order 16384. Some front has 256 pivots.
All inputs are finite; a program needn't handle non-finite values.
Results may differ from the reference program's by a relative error of at most 0.0003.
Values sent between devices are 32-bit elements; how exact they have to be, the bound alone decides.
No kernel may reach another device: no remote copies, remote signals or barrier semaphores. Data moves between devices by JAX's collectives and lax.ppermute only.
A program may use at most 192 MiB of HBM per device.

```python
import math
import jax
import jax.numpy as jnp
from jax import lax

FRONT = 16384
BLK = 128
PW = 256
CH_DEV = 2
CROWS = 2048
NCOL = 512
NPIV = 256
ROW_BLOCK_CYCLE = 32
CRC = 4
CRB = 16
FRONTS = 32
CHILDREN = 64


def force_entry(perm, source, target):
    holder = jnp.argmax(perm == target).astype(jnp.int32)
    former = perm[source]
    perm = perm.at[holder].set(former)
    return perm.at[source].set(target)


def tree_layout(key):
    key = jax.random.fold_in(key, 7)
    k_order, k_top, k_perm, k_shift, k_maps, k_start = jax.random.split(key, 6)
    full_blocks = FRONT // BLK
    order_blocks = jax.random.randint(k_order, (FRONTS,), full_blocks // 2, full_blocks + 1)
    top_front = jax.random.randint(k_top, (), 0, FRONTS)
    order_blocks = jnp.where(jnp.arange(FRONTS) == top_front, full_blocks, order_blocks)
    perm = jax.random.permutation(k_perm, FRONTS).astype(jnp.int32)
    start_at = jax.random.randint(k_start, (), 0, FRONTS).astype(jnp.int32)
    perm = force_entry(perm, start_at, (start_at + 1) % FRONTS)
    second = (start_at + 2) % FRONTS
    perm = force_entry(perm, second, (second + FRONTS // 2) % FRONTS)
    offset = jax.random.randint(k_shift, (), 1, FRONTS).astype(jnp.int32)
    slot_ids = (perm[:, None] + jnp.arange(CH_DEV, dtype=jnp.int32)[None, :] * offset) % FRONTS
    parent_ids = slot_ids.reshape(CHILDREN).astype(jnp.int32)
    rows_axis = FRONT // (BLK * ROW_BLOCK_CYCLE)
    child_cycles = CROWS // (BLK * rows_axis)
    cycle_index_list = jnp.arange(ROW_BLOCK_CYCLE, dtype=jnp.int32)
    residues = jnp.arange(rows_axis, dtype=jnp.int32)
    block_ids = cycle_index_list[None, :] * rows_axis + residues[:, None]
    limits = order_blocks[parent_ids]
    eligible_flags = block_ids[None, :, :] < limits[:, None, None]
    random_jitter = jax.random.randint(k_maps, (CHILDREN, rows_axis, ROW_BLOCK_CYCLE), 0, 1 << 16)
    final_complete = (limits[:, None, None] == full_blocks) & (cycle_index_list[None, None, :] == ROW_BLOCK_CYCLE - 1)
    extra_credit = jnp.where(final_complete, (1 << 17) * ROW_BLOCK_CYCLE, 0)
    rating_values = jnp.where(eligible_flags, random_jitter * ROW_BLOCK_CYCLE + cycle_index_list[None, None, :] + 1 + extra_credit, -(cycle_index_list[None, None, :] + 1))
    chosen = lax.top_k(rating_values, child_cycles)[1].astype(jnp.int32)
    mapped = chosen * rows_axis + residues[None, :, None]
    mapped = jnp.transpose(mapped, (0, 2, 1)).reshape(CHILDREN, CRB)
    return (order_blocks * BLK, parent_ids, mapped)


def draw_parents(key, part):
    order_rows, parent_ids, mapped = tree_layout(key)
    return parent_ids


def draw_row_maps(key, part):
    order_rows, parent_ids, mapped = tree_layout(key)
    return mapped


def draw_orders(key, part):
    order_rows, parent_ids, mapped = tree_layout(key)
    return order_rows.astype(jnp.int32)


def draw_pivots(key, part):
    key = jax.random.fold_in(key, 11)
    k_count, k_top = jax.random.split(key)
    counts = jax.random.randint(k_count, (FRONTS,), 1, NPIV + 1)
    top_front = jax.random.randint(k_top, (), 0, FRONTS)
    counts = jnp.where(jnp.arange(FRONTS) == top_front, NPIV, counts)
    return counts.astype(jnp.int32)


def draw_children(key, part):
    order_rows, parent_ids, mapped = tree_layout(key)
    key = jax.random.fold_in(key, 13)
    values = jax.random.truncated_normal(key, -6.0, 6.0, (CHILDREN, CROWS, NCOL), jnp.float32)
    child_blocks = jnp.arange(CROWS, dtype=jnp.int32) // BLK
    target = mapped[:, child_blocks]
    scales = jnp.where(target * BLK < NCOL, 0.5 / math.sqrt(NCOL), 0.5)
    values = values * scales[:, :, None]
    return values.reshape(CHILDREN, CRC, CROWS // CRC, NCOL)


def draw_panel(key, part):
    key = jax.random.fold_in(key, 17)
    k_normal, k_diag = jax.random.split(key)
    values = jax.random.truncated_normal(k_normal, -6.0, 6.0, (FRONTS, FRONT, NCOL), jnp.float32)
    diagonal = jax.random.uniform(k_diag, (FRONTS, FRONT, NCOL), jnp.float32, 6.0, 12.0)
    row_ids = jnp.arange(FRONT, dtype=jnp.int32)[:, None]
    col_ids = jnp.arange(NCOL, dtype=jnp.int32)[None, :]
    upper_part = values / math.sqrt(NCOL) + jnp.where(row_ids == col_ids, diagonal, 0.0)
    values = jnp.where(row_ids < NCOL, upper_part, values)
    return values.reshape(FRONTS, ROW_BLOCK_CYCLE, FRONT // ROW_BLOCK_CYCLE, NCOL)


def setup_inputs(seed: int = 0) -> dict:
    streams_of = jax.random.split(jax.random.key(seed), 7)
    return {
        "panel": draw_panel(jax.random.fold_in(streams_of[6], 71), 0),
        "children": draw_children(jax.random.fold_in(streams_of[6], 71), 0),
        "parents": draw_parents(jax.random.fold_in(streams_of[6], 71), 0),
        "row_maps": draw_row_maps(jax.random.fold_in(streams_of[6], 71), 0),
        "orders": draw_orders(jax.random.fold_in(streams_of[6], 71), 0),
        "pivots": draw_pivots(jax.random.fold_in(streams_of[6], 71), 0),
    }


def factor_front(inputs):
    front_block, order_rows, pivot_count = inputs
    row_ids = jnp.arange(FRONT, dtype=jnp.int32)[:, None]
    col_ids = jnp.arange(NCOL, dtype=jnp.int32)[None, :]
    keep_mask = (row_ids >= col_ids) & (row_ids < order_rows)
    current = jnp.where(keep_mask, front_block, jnp.zeros_like(front_block))
    for panel_at in range(NPIV // PW):
        first_col = panel_at * PW
        active = (first_col + jnp.arange(PW, dtype=jnp.int32) < pivot_count).astype(front_block.dtype)
        corner = current[first_col:first_col + PW, first_col:first_col + PW]
        diag_rows = jnp.tril(corner) + jnp.tril(corner, -1).T
        masked = diag_rows * active[:, None] * active[None, :] + jnp.diag(1.0 - active)
        factor = jnp.linalg.cholesky(masked)
        filled = current[:, first_col:first_col + PW].at[first_col:first_col + PW].set(diag_rows)
        panel_l = lax.linalg.triangular_solve(factor, filled * active[None, :], left_side=False, lower=True, transpose_a=True)
        panel_l = jnp.where(row_ids >= first_col, panel_l, jnp.zeros_like(panel_l))
        update = jnp.dot(panel_l, panel_l[:NCOL].T, precision=lax.Precision.HIGHEST)
        current = jnp.where(col_ids >= first_col, current - update, current)
        old_cols = current[:, first_col:first_col + PW]
        current = current.at[:, first_col:first_col + PW].set(jnp.where(active[None, :] > 0, panel_l, old_cols))
    return jnp.where(keep_mask, current, jnp.zeros_like(current))

def reference(panel, children, parents, row_maps, orders, pivots):
    fronts_view = panel.reshape(FRONTS, FRONT // BLK, BLK, NCOL)
    child_blocks = children.reshape(CHILDREN, CROWS // BLK, BLK, NCOL)
    assembled = fronts_view.at[parents[:, None], row_maps].add(child_blocks)
    assembled = assembled.reshape(FRONTS, FRONT, NCOL)
    factored = lax.map(factor_front, (assembled, orders, pivots))
    return factored.reshape(panel.shape)
```

```python
import jax
import jax.numpy as jnp
from jax import lax
from jax.experimental import pallas as pl
from jax.experimental.pallas import tpu as pltpu
from jax.sharding import PartitionSpec as P

F32 = jnp.float32
BLOCK = 128
WIDTH = 256
BASE = 32
VMEM = pl.BlockSpec(memory_space=pltpu.VMEM)
SMEM = pl.BlockSpec(memory_space=pltpu.SMEM)


def dot(a, b, ca=1, cb=0):
    return lax.dot_general(
        a, b, (((ca,), (cb,)), ((), ())),
        precision=lax.Precision.HIGHEST, preferred_element_type=F32,
    )


def targets_of(maps_ref, child, row, rows):
    cycles = maps_ref.shape[1] // rows
    targets = [maps_ref[child, rows * i + row] // rows for i in range(cycles)]
    first = jnp.int32(0)
    found = jnp.int32(0)
    for i in range(cycles):
        hit = targets[i] == 0
        first = jnp.where(hit, i, first)
        found = jnp.where(hit, 1, found)
    return targets, first, found


def slot_block(slot, first):
    if slot == 0:
        return first
    return jnp.where(first >= slot, slot - 1, slot)


def pick(values, at):
    out = values[0]
    for i in range(1, len(values)):
        out = jnp.where(at == i, values[i], out)
    return out


def child_of(parents_ref, front, which):
    found = jnp.int32(0)
    for d in range(parents_ref.shape[0] // 2):
        found = jnp.where(parents_ref[2 * d + which] == front, 2 * d + which, found)
    return found


def spread_kernel(maps_ref, children_ref, out_ref, *, rows):
    front, row = lax.axis_index("front"), lax.axis_index("row")
    cycles = children_ref.shape[1]
    for c in range(2):
        _, first, _ = targets_of(maps_ref, 2 * front + c, row, rows)
        for s in range(cycles):
            block = slot_block(s, first)
            at = (c * cycles + s) * 8
            for half in range(2):
                tiles = children_ref[c, block, :, half * 128:(half + 1) * 128]
                out_ref[:, half, at:at + 8, :] = tiles.reshape(BLOCK // 8, 8, 128)


def route_kernel(parents_ref, in_ref, first_ref, rest_ref):
    fronts, depth = in_ref.shape[0], in_ref.shape[1]
    half = depth // 2
    for d in range(fronts):
        for c in range(2):
            to = parents_ref[2 * d + c]
            first_ref[to, c * 8:(c + 1) * 8, :] = in_ref[d, c * half:c * half + 8, :]
            rest_ref[to, c * (half - 8):(c + 1) * (half - 8), :] = in_ref[
                d, c * half + 8:(c + 1) * half, :
            ]


def tile_block(ref, at):
    return jnp.concatenate(
        [ref[:, half, at:at + 8, :].reshape(BLOCK, 128) for half in range(2)], axis=1
    )


def top_kernel(parents_ref, maps_ref, panel_ref, first_ref, out_ref, *, rows):
    front, row = lax.axis_index("front"), lax.axis_index("row")
    total = panel_ref[0]
    for c in range(2):
        child = child_of(parents_ref, front, c)
        _, _, found = targets_of(maps_ref, child, row, rows)
        total = total + tile_block(first_ref, c * 8) * found.astype(F32)
    out_ref[...] = total


def invert_base(a):
    n = a.shape[0]
    r = lax.broadcasted_iota(jnp.int32, (n, n), 0)
    l = lax.broadcasted_iota(jnp.int32, (n, n), 1)
    t = jnp.where(r == l, 1.0, 0.0).astype(F32)
    rows = lax.broadcasted_iota(jnp.int32, (n, 1), 0)
    for j in range(n - 1):
        f = jnp.where(rows > j, a[:, j:j + 1] / a[j:j + 1, j:j + 1], 0.0)
        a = a - f * a[j:j + 1, :]
        t = t - f * t[j:j + 1, :]
    d = jnp.sum(jnp.where(r == l, a, 0.0), axis=1, keepdims=True)
    return t * lax.rsqrt(d)


def invert_factor(a):
    n = a.shape[0]
    if n == BASE:
        return invert_base(a)
    h = n // 2
    w1 = invert_factor(a[:h, :h])
    l21 = dot(a[h:, :h], w1, 1, 1)
    w2 = invert_factor(a[h:, h:] - dot(l21, l21, 1, 1))
    w21 = -dot(w2, dot(l21, w1))
    return jnp.concatenate(
        [
            jnp.concatenate([w1, jnp.zeros((h, h), F32)], axis=1),
            jnp.concatenate([w21, w2], axis=1),
        ],
        axis=0,
    )


def factor_kernel(pivots_ref, own_ref, r1_ref, r2_ref, r3_ref, solve_ref, send_ref, all_ref):
    row = lax.axis_index("row")
    for s, ref in enumerate((own_ref, r1_ref, r2_ref, r3_ref)):
        at = pl.multiple_of(lax.rem(row + 4 - s, 4) * BLOCK, BLOCK)
        all_ref[pl.ds(at, BLOCK), :] = ref[...]
    pivots = pivots_ref[0]
    r = lax.broadcasted_iota(jnp.int32, (WIDTH, WIDTH), 0)
    l = lax.broadcasted_iota(jnp.int32, (WIDTH, WIDTH), 1)
    both = (r < pivots) & (l < pivots)
    diag = all_ref[0:WIDTH, :]
    low = jnp.where(r >= l, diag, 0.0)
    strict = jnp.where(r > l, diag, 0.0)
    mirrored = low + strict.T
    masked = jnp.where(both, mirrored, jnp.where(r == l, 1.0, 0.0))
    inverse = jnp.where(both, invert_factor(masked), 0.0)
    solved = dot(all_ref[...], inverse, 1, 1)
    top = jnp.where(r >= l, solved[:WIDTH], 0.0)
    solve_t = inverse - jnp.where(r < pivots, 0.0, dot(top, inverse))
    update_t = dot(solved[WIDTH:], inverse)
    solve_ref[...] = solve_t.T
    send_ref[0:WIDTH, :] = update_t.T
    send_ref[WIDTH:, :] = own_ref[...]


def main_kernel(orders_ref, pivots_ref, panel_ref, left_ref, top_ref, solve_ref, sent_ref, out_ref, *, rows):
    row, col = lax.axis_index("row"), lax.axis_index("col")
    step = pl.program_id(0)
    cycles = panel_ref.shape[0]
    orders, pivots = orders_ref[0], pivots_ref[0]
    lane = lax.broadcasted_iota(jnp.int32, (1, WIDTH), 1)
    rest = jnp.where(lane < pivots, 0.0, 1.0)
    first = step == 0
    x0 = jnp.where(first, top_ref[...], panel_ref[0])

    @pl.when(col == 0)
    def _():
        x = jnp.concatenate([x0] + [panel_ref[i] for i in range(1, cycles)], axis=0)
        y = dot(x, solve_ref[...]) + x * rest
        for i in range(cycles):
            out_ref[i] = y[i * BLOCK:(i + 1) * BLOCK]

    @pl.when(col != 0)
    def _():
        z0 = jnp.where(first, sent_ref[WIDTH:, :], left_ref[0])
        x = jnp.concatenate([z0] + [left_ref[i] for i in range(1, cycles)], axis=0)
        y = dot(x, sent_ref[0:WIDTH, :])
        out_ref[0] = x0 - y[:BLOCK]
        for i in range(1, cycles):
            out_ref[i] = panel_ref[i] - y[i * BLOCK:(i + 1) * BLOCK]

    for i in range(cycles):
        start = ((step * cycles + i) * rows + row) * BLOCK

        @pl.when(start >= orders)
        def _():
            out_ref[i] = jnp.zeros((BLOCK, WIDTH), F32)

    @pl.when(first)
    def _():
        g = row * BLOCK + lax.broadcasted_iota(jnp.int32, (BLOCK, WIDTH), 0)
        j = col * WIDTH + lax.broadcasted_iota(jnp.int32, (BLOCK, WIDTH), 1)
        out_ref[0] = jnp.where(g >= j, out_ref[0], 0.0)


def late_kernel(parents_ref, maps_ref, pivots_ref, first_ref, rest_ref, lfirst_ref, lrest_ref,
                solve_ref, sent_ref, base_ref, out_ref, hold_ref, sem_in, sem_out, *, rows):
    front, row, col = lax.axis_index("front"), lax.axis_index("row"), lax.axis_index("col")
    cycles = maps_ref.shape[1] // rows
    pivots = pivots_ref[0]
    lane = lax.broadcasted_iota(jnp.int32, (1, WIDTH), 1)
    rest = jnp.where(lane < pivots, 0.0, 1.0)
    for c in range(2):
        child = child_of(parents_ref, front, c)
        targets, first, found = targets_of(maps_ref, child, row, rows)
        place = [pick(targets, slot_block(s, first)) for s in range(cycles)]
        for s in range(cycles):
            @pl.when(place[s] != 0)
            def _():
                pltpu.make_async_copy(base_ref.at[place[s]], hold_ref.at[s], sem_in.at[s]).start()
        for s in range(cycles):
            at = c * 8 if s == 0 else (c * (cycles - 1) + s - 1) * 8
            mine, left = (first_ref, lfirst_ref) if s == 0 else (rest_ref, lrest_ref)

            @pl.when(place[s] != 0)
            def _():
                pltpu.make_async_copy(base_ref.at[place[s]], hold_ref.at[s], sem_in.at[s]).wait()

                @pl.when(col == 0)
                def _():
                    x = tile_block(mine, at)
                    hold_ref[s] = hold_ref[s] + x * rest + dot(x, solve_ref[...])

                @pl.when(col != 0)
                def _():
                    hold_ref[s] = hold_ref[s] + tile_block(mine, at) - dot(
                        tile_block(left, at), sent_ref[0:WIDTH, :]
                    )

                pltpu.make_async_copy(hold_ref.at[s], out_ref.at[place[s]], sem_out.at[s]).start()
        for s in range(cycles):
            @pl.when(place[s] != 0)
            def _():
                pltpu.make_async_copy(hold_ref.at[s], out_ref.at[place[s]], sem_out.at[s]).wait()


def on_device(panel, children, parents, row_maps, orders, pivots):
    rows = lax.axis_size("row")
    fronts = lax.axis_size("front")
    cycles = panel.shape[1]
    child_cycles = children.shape[1]
    panel = panel[0]
    depth = 2 * child_cycles * 8
    params = pltpu.CompilerParams(vmem_limit_bytes=40 * 2**20)

    to_right = [(0, 1)]
    left = lax.ppermute(panel, "col", to_right)

    spread = pl.pallas_call(
        lambda *refs: spread_kernel(*refs, rows=rows),
        out_shape=jax.ShapeDtypeStruct((BLOCK // 8, 2, depth, 128), F32),
        in_specs=[SMEM, VMEM], out_specs=VMEM, compiler_params=params, name="spread",
    )(row_maps, children)
    spread = lax.all_to_all(spread.reshape(fronts, depth, 128), "front", 0, 0, tiled=True)
    first, rest = pl.pallas_call(
        route_kernel,
        out_shape=(
            jax.ShapeDtypeStruct((fronts, 16, 128), F32),
            jax.ShapeDtypeStruct((fronts, depth - 16, 128), F32),
        ),
        in_specs=[SMEM, VMEM], out_specs=(VMEM, VMEM), compiler_params=params, name="route",
    )(parents, spread)
    first = lax.all_to_all(first, "front", 0, 0, tiled=True)
    rest, first = lax.optimization_barrier((rest, first))
    rest = lax.all_to_all(rest, "front", 0, 0, tiled=True)
    pieces = (BLOCK // 8, 2)
    first = first.reshape(*pieces, 16, 128)
    rest = rest.reshape(*pieces, depth - 16, 128)

    top = pl.pallas_call(
        lambda *refs: top_kernel(*refs, rows=rows),
        grid=(1,),
        out_shape=jax.ShapeDtypeStruct((BLOCK, WIDTH), F32),
        in_specs=[
            SMEM, SMEM,
            pl.BlockSpec((1, BLOCK, WIDTH), lambda i: (0, 0, 0)),
            pl.BlockSpec((*pieces, 16, 128), lambda i: (0, 0, 0, 0)),
        ],
        out_specs=pl.BlockSpec((BLOCK, WIDTH), lambda i: (0, 0)),
        compiler_params=params, name="top",
    )(parents, row_maps, panel, first)
    others = [
        lax.ppermute(top, "row", [(i, (i + s) % rows) for i in range(rows)]) for s in (1, 2, 3)
    ]
    solve, send = pl.pallas_call(
        factor_kernel,
        out_shape=(
            jax.ShapeDtypeStruct((WIDTH, WIDTH), F32),
            jax.ShapeDtypeStruct((WIDTH + BLOCK, WIDTH), F32),
        ),
        in_specs=[SMEM, VMEM, VMEM, VMEM, VMEM], out_specs=(VMEM, VMEM),
        scratch_shapes=[pltpu.VMEM((4 * BLOCK, WIDTH), F32)],
        compiler_params=params, name="factor",
        cost_estimate=pl.CostEstimate(flops=2 * 10**9, bytes_accessed=2**21, transcendentals=0),
    )(pivots, top, *others)
    sent = lax.ppermute(send, "col", to_right)
    left_first = lax.ppermute(first, "col", to_right)

    per = 4
    chunk = pl.BlockSpec((per, BLOCK, WIDTH), lambda i: (i, 0, 0))
    whole = lambda *shape: pl.BlockSpec(shape, lambda i: (0,) * len(shape))
    base = pl.pallas_call(
        lambda *refs: main_kernel(*refs, rows=rows),
        grid=(cycles // per,),
        out_shape=jax.ShapeDtypeStruct(panel.shape, F32),
        in_specs=[
            SMEM, SMEM, chunk, chunk,
            whole(BLOCK, WIDTH), whole(WIDTH, WIDTH), whole(WIDTH + BLOCK, WIDTH),
        ],
        out_specs=chunk, compiler_params=params, name="main",
        cost_estimate=pl.CostEstimate(flops=10**9, bytes_accessed=12 * 2**20, transcendentals=0),
    )(orders, pivots, panel, left, top, solve, sent)

    left_rest = lax.ppermute(rest, "col", to_right)
    hbm = pl.BlockSpec(memory_space=pl.ANY)
    out = pl.pallas_call(
        lambda *refs: late_kernel(*refs, rows=rows),
        out_shape=jax.ShapeDtypeStruct(panel.shape, F32),
        in_specs=[SMEM, SMEM, SMEM, VMEM, VMEM, VMEM, VMEM, VMEM, VMEM, hbm],
        out_specs=hbm,
        scratch_shapes=[
            pltpu.VMEM((child_cycles, BLOCK, WIDTH), F32),
            pltpu.SemaphoreType.DMA((child_cycles,)),
            pltpu.SemaphoreType.DMA((child_cycles,)),
        ],
        input_output_aliases={9: 0},
        compiler_params=params, name="late",
        cost_estimate=pl.CostEstimate(flops=10**8, bytes_accessed=4 * 2**20, transcendentals=0),
    )(parents, row_maps, pivots, first, rest, left_first, left_rest, solve, sent, base)
    return out[None]


def solution(mesh):
    in_specs = (
        P("front", None, "row", "col"),
        P("front", None, "row", "col"),
        P(),
        P(),
        P("front"),
        P("front"),
    )
    out_specs = P("front", None, "row", "col")
    return jax.shard_map(
        on_device, mesh=mesh, in_specs=in_specs, out_specs=out_specs, check_vma=False
    )
```

```python
import jax
import jax.numpy as jnp
from jax import lax
from jax.experimental import pallas as pl
from jax.experimental.pallas import tpu as pltpu
from jax.sharding import PartitionSpec as P

F32 = jnp.float32
BLOCK = 128
WIDTH = 256
BASE = 64
GROUP = 16
CHUNK = 8
VMEM = pl.BlockSpec(memory_space=pltpu.VMEM)
HBM = pl.BlockSpec(memory_space=pltpu.HBM)
SMEM = pl.BlockSpec(memory_space=pltpu.SMEM)


def dot(a, b, ca=1, cb=0):
    return lax.dot_general(
        a, b, (((ca,), (cb,)), ((), ())),
        precision=lax.Precision.HIGHEST, preferred_element_type=F32,
    )


def split(a):
    high = a.astype(jnp.bfloat16)
    return high, (a - high.astype(F32)).astype(jnp.bfloat16)


def dot_split(a, b):
    def part(x, y):
        return lax.dot_general(x, y, (((1,), (0,)), ((), ())), preferred_element_type=F32)

    (ah, al), (bh, bl) = split(a), b
    return part(ah, bh) + (part(ah, bl) + part(al, bh))


def targets_of(maps_ref, child, row, rows):
    cycles = maps_ref.shape[1] // rows
    targets = [maps_ref[child, rows * i + row] // rows for i in range(cycles)]
    first = jnp.int32(0)
    found = jnp.int32(0)
    for i in range(cycles):
        hit = targets[i] == 0
        first = jnp.where(hit, i, first)
        found = jnp.where(hit, 1, found)
    return targets, first, found


def slot_block(slot, first):
    if slot == 0:
        return first
    return jnp.where(first >= slot, slot - 1, slot)


def pick(values, at):
    out = values[0]
    for i in range(1, len(values)):
        out = jnp.where(at == i, values[i], out)
    return out


def child_of(parents_ref, front, which):
    found = jnp.int32(0)
    for d in range(parents_ref.shape[0] // 2):
        found = jnp.where(parents_ref[2 * d + which] == front, 2 * d + which, found)
    return found


def spread_kernel(maps_ref, children_ref, out_ref, hold_ref, targets_ref, sem_maps, sem, *, rows):
    front, row = lax.axis_index("front"), lax.axis_index("row")
    maps = pltpu.make_async_copy(maps_ref, targets_ref, sem_maps)
    maps.start()
    copies = [
        pltpu.make_async_copy(children_ref.at[c], hold_ref.at[c], sem.at[c]) for c in range(2)
    ]
    for copy in copies:
        copy.start()
    cycles = children_ref.shape[1]
    maps.wait()
    for c in range(2):
        _, first, _ = targets_of(targets_ref, 2 * front + c, row, rows)
        copies[c].wait()
        for s in range(cycles):
            at = (c * cycles + s) * 8
            for half in range(2):
                tiles = hold_ref[c, slot_block(s, first), :, half * 128:(half + 1) * 128]
                out_ref[:, half, at:at + 8, :] = tiles.reshape(BLOCK // 8, 8, 128)


def route_kernel(parents_ref, in_ref, first_ref, rest_ref):
    fronts, depth = in_ref.shape[0], in_ref.shape[1]
    half = depth // 2
    for d in range(fronts):
        for c in range(2):
            to = parents_ref[2 * d + c]
            first_ref[to, c * 8:(c + 1) * 8, :] = in_ref[d, c * half:c * half + 8, :]
            rest_ref[to, c * (half - 8):(c + 1) * (half - 8), :] = in_ref[
                d, c * half + 8:(c + 1) * half, :
            ]


def tile_block(ref, at):
    return jnp.concatenate(
        [ref[:, half, at:at + 8, :].reshape(BLOCK, 128) for half in range(2)], axis=1
    )


def top_kernel(parents_ref, maps_ref, panel_ref, pieces_ref, out_ref, first_ref, *, rows):
    front, row = lax.axis_index("front"), lax.axis_index("row")
    total = panel_ref[...]
    for c in range(2):
        first_ref[c] = tile_block(pieces_ref, c * 8)
        child = child_of(parents_ref, front, c)
        total += first_ref[c] * targets_of(maps_ref, child, row, rows)[2].astype(F32)
    out_ref[...] = total


def invert_base(a):
    n = a.shape[0]
    r = lax.broadcasted_iota(jnp.int32, (n, n), 0)
    l = lax.broadcasted_iota(jnp.int32, (n, n), 1)
    both = jnp.concatenate([a, jnp.where(r == l, 1.0, 0.0).astype(F32)], axis=1)
    done = []
    for g in range(0, n, GROUP):
        below = n - g
        sub = lax.broadcasted_iota(jnp.int32, (below, 2 * n), 0)
        columns = [
            jnp.broadcast_to(both[:, g + q:g + q + 1], (below, 2 * n)) for q in range(GROUP)
        ]
        diag = jnp.ones((GROUP, 2 * n), F32)
        for q in range(GROUP):
            column = columns[q]
            pivot = column[q:q + 1, :]
            diag = jnp.where(sub[:GROUP] == q, pivot, diag)
            f = jnp.where(sub > q, column, 0.0) * (1.0 / pivot)
            for k in range(q + 1, GROUP):
                columns[k] = columns[k] - f * columns[k][q:q + 1, :]
            both = both - f * both[q:q + 1, :]
        done.append(both[:GROUP] * lax.rsqrt(diag))
        both = both[GROUP:]
    return jnp.concatenate(done, axis=0)[:, n:]


def invert_factor(a):
    n = a.shape[0]
    if n == BASE:
        return invert_base(a)
    h = n // 2
    w1 = invert_factor(a[:h, :h])
    l21 = dot(a[h:, :h], w1, 1, 1)
    w2 = invert_factor(a[h:, h:] - dot(l21, l21, 1, 1))
    w21 = -dot(w2, dot(l21, w1))
    return jnp.concatenate(
        [
            jnp.concatenate([w1, jnp.zeros((h, h), F32)], axis=1),
            jnp.concatenate([w21, w2], axis=1),
        ],
        axis=0,
    )


def factor_kernel(pivots_ref, own_ref, r1_ref, r2_ref, r3_ref, solve_ref, send_ref, all_ref):
    row = lax.axis_index("row")
    for s, ref in enumerate((own_ref, r1_ref, r2_ref, r3_ref)):
        at = pl.multiple_of(lax.rem(row + 4 - s, 4) * BLOCK, BLOCK)
        all_ref[pl.ds(at, BLOCK), :] = ref[...]
    pivots = pivots_ref[0]
    r = lax.broadcasted_iota(jnp.int32, (WIDTH, WIDTH), 0)
    l = lax.broadcasted_iota(jnp.int32, (WIDTH, WIDTH), 1)
    both = (r < pivots) & (l < pivots)
    diag = all_ref[0:WIDTH, :]
    low = jnp.where(r >= l, diag, 0.0)
    strict = jnp.where(r > l, diag, 0.0)
    mirrored = low + strict.T
    masked = jnp.where(both, mirrored, jnp.where(r == l, 1.0, 0.0))
    inverse = jnp.where(both, invert_factor(masked), 0.0)
    solved = dot(all_ref[...], inverse, 1, 1)
    top = jnp.where(r >= l, solved[:WIDTH], 0.0)
    solve_t = inverse - jnp.where(r < pivots, 0.0, dot(top, inverse))
    update_t = dot(solved[WIDTH:], inverse)
    solve_ref[...] = solve_t.T
    send_ref[0:WIDTH, :] = update_t.T
    send_ref[WIDTH:, :] = own_ref[...]


def finish_kernel(parents_ref, maps_ref, orders_ref, pivots_ref, top_ref, solve_ref, sent_ref,
                  first_ref, rest_ref, lfirst_ref, lrest_ref, panel_ref, left_ref, out_ref,
                  hold_ref, x_ref, sem_hold, sem_x, sem_out, *, rows):
    front, row, col = lax.axis_index("front"), lax.axis_index("row"), lax.axis_index("col")
    cycles = panel_ref.shape[0]
    child_cycles = maps_ref.shape[1] // rows
    orders, pivots = orders_ref[0], pivots_ref[0]
    chunks = [pl.ds(k, CHUNK) for k in range(0, cycles, CHUNK)]
    hold = [
        pltpu.make_async_copy(panel_ref.at[at], hold_ref.at[at], sem_hold.at[k])
        for k, at in enumerate(chunks)
    ]
    store = [
        pltpu.make_async_copy(hold_ref.at[at], out_ref.at[at], sem_out.at[k])
        for k, at in enumerate(chunks)
    ]
    for k, at in enumerate(chunks):
        hold[k].start()

        @pl.when(col == 0)
        def _():
            pltpu.make_async_copy(panel_ref.at[at], x_ref.at[at], sem_x.at[k]).start()

        @pl.when(col != 0)
        def _():
            pltpu.make_async_copy(left_ref.at[at], x_ref.at[at], sem_x.at[k]).start()

    places = []
    for c in range(2):
        targets, first, _ = targets_of(maps_ref, child_of(parents_ref, front, c), row, rows)
        for s in range(child_cycles):
            places.append((pick(targets, slot_block(s, first)), c, s))

    def child_block(first, rest, c, s):
        if s == 0:
            return first[c]
        return tile_block(rest, (c * (child_cycles - 1) + s - 1) * 8)

    lane = lax.broadcasted_iota(jnp.int32, (1, WIDTH), 1)
    scale = jnp.where((col != 0) | (lane >= pivots), 1.0, 0.0)
    right = split(jnp.where(col == 0, solve_ref[...], -sent_ref[0:WIDTH, :]))
    for k, at in enumerate(chunks):
        hold[k].wait()
        pltpu.make_async_copy(panel_ref.at[at], x_ref.at[at], sem_x.at[k]).wait()
        if k == 0:
            hold_ref[0] = top_ref[...]
            x_ref[0] = jnp.where(col == 0, top_ref[...], sent_ref[WIDTH:, :])
        for place, c, s in places:
            @pl.when((place != 0) & (place // CHUNK == k))
            def _():
                hold_ref[place] += child_block(first_ref, rest_ref, c, s)

                @pl.when(col == 0)
                def _():
                    x_ref[place] += child_block(first_ref, rest_ref, c, s)

                @pl.when(col != 0)
                def _():
                    x_ref[place] += child_block(lfirst_ref, lrest_ref, c, s)

        y = dot_split(x_ref[at].reshape(CHUNK * BLOCK, WIDTH), right)
        for i in range(CHUNK):
            cycle = k * CHUNK + i
            start = (cycle * rows + row) * BLOCK
            z = hold_ref[cycle] * scale + y[i * BLOCK:(i + 1) * BLOCK]
            keep = start < orders
            if cycle == 0:
                g = row * BLOCK + lax.broadcasted_iota(jnp.int32, (BLOCK, WIDTH), 0)
                j = col * WIDTH + lax.broadcasted_iota(jnp.int32, (BLOCK, WIDTH), 1)
                keep = keep & (g >= j)
            hold_ref[cycle] = jnp.where(keep, z, 0.0)
        store[k].start()
    for copy in store:
        copy.wait()


def on_device(panel, children, parents, row_maps, orders, pivots):
    rows = lax.axis_size("row")
    fronts = lax.axis_size("front")
    cycles = panel.shape[1]
    child_cycles = children.shape[1]
    panel = panel[0]
    depth = 2 * (child_cycles - 1) * 8
    pieces = (BLOCK // 8, 2)
    params = pltpu.CompilerParams(vmem_limit_bytes=32 * 2**20)
    shape = lambda *dims: jax.ShapeDtypeStruct(dims, F32)
    to_right = [(0, 1)]

    def exchange(value):
        return lax.all_to_all(value.reshape(fronts, -1, 128), "front", 0, 0, tiled=True)

    spread = pl.pallas_call(
        lambda *refs: spread_kernel(*refs, rows=rows),
        out_shape=shape(*pieces, depth + 16, 128),
        in_specs=[HBM, HBM], out_specs=VMEM,
        scratch_shapes=[
            pltpu.VMEM(children.shape, F32), pltpu.SMEM(row_maps.shape, jnp.int32),
            pltpu.SemaphoreType.DMA, pltpu.SemaphoreType.DMA((2,)),
        ],
        compiler_params=pltpu.CompilerParams(vmem_limit_bytes=62 * 2**20), name="spread",
    )(row_maps, children)
    spread = exchange(spread)
    first, rest = pl.pallas_call(
        route_kernel, out_shape=(shape(fronts, 16, 128), shape(fronts, depth, 128)),
        in_specs=[SMEM, VMEM], out_specs=(VMEM, VMEM), compiler_params=params, name="route",
    )(parents, spread)
    first, panel = lax.optimization_barrier((first, panel))
    left = lax.ppermute(panel, "col", to_right)
    first = exchange(first)
    panel_top = panel[0]
    top, first = pl.pallas_call(
        lambda *refs: top_kernel(*refs, rows=rows),
        out_shape=(shape(BLOCK, WIDTH), shape(2, BLOCK, WIDTH)),
        in_specs=[SMEM, SMEM, VMEM, VMEM], out_specs=(VMEM, VMEM),
        compiler_params=params, name="top",
    )(parents, row_maps, panel_top, first.reshape(*pieces, 16, 128))
    rest, top = lax.optimization_barrier((rest, top))
    rest = exchange(rest).reshape(*pieces, depth, 128)
    others = [
        lax.ppermute(top, "row", [(i, (i + s) % rows) for i in range(rows)]) for s in (1, 2, 3)
    ]
    left_first = lax.ppermute(first, "col", to_right)
    *others, left_first = lax.optimization_barrier((*others, left_first))
    solve, send = pl.pallas_call(
        factor_kernel,
        out_shape=(shape(WIDTH, WIDTH), shape(WIDTH + BLOCK, WIDTH)),
        in_specs=[SMEM, VMEM, VMEM, VMEM, VMEM], out_specs=(VMEM, VMEM),
        scratch_shapes=[pltpu.VMEM((4 * BLOCK, WIDTH), F32)],
        compiler_params=params, name="factor",
        cost_estimate=pl.CostEstimate(flops=2 * 10**9, bytes_accessed=2**21, transcendentals=0),
    )(pivots, top, *others)
    sent = lax.ppermute(send, "col", to_right)

    rest, solve = lax.optimization_barrier((rest, solve))
    left_rest = lax.ppermute(rest, "col", to_right)
    steps = cycles // CHUNK
    out = pl.pallas_call(
        lambda *refs: finish_kernel(*refs, rows=rows),
        out_shape=shape(*panel.shape),
        in_specs=[SMEM] * 4 + [VMEM] * 7 + [HBM] * 2, out_specs=HBM,
        scratch_shapes=[pltpu.VMEM(panel.shape, F32)] * 2 + [pltpu.SemaphoreType.DMA((steps,))] * 3,
        compiler_params=pltpu.CompilerParams(vmem_limit_bytes=57 * 2**20), name="finish",
        cost_estimate=pl.CostEstimate(flops=10**9, bytes_accessed=12 * 2**20, transcendentals=0),
    )(
        parents, row_maps, orders, pivots, top, solve, sent,
        first, rest, left_first, left_rest, panel, left,
    )
    return out[None]


def solution(mesh):
    in_specs = (
        P("front", None, "row", "col"),
        P("front", None, "row", "col"),
        P(),
        P(),
        P("front"),
        P("front"),
    )
    out_specs = P("front", None, "row", "col")
    return jax.shard_map(
        on_device, mesh=mesh, in_specs=in_specs, out_specs=out_specs, check_vma=False
    )
```

```python
import jax
import jax.numpy as jnp
from jax import lax
from jax.experimental import pallas as pl
from jax.experimental.pallas import tpu as pltpu
from jax.sharding import PartitionSpec as P

F32 = jnp.float32
BLOCK = 128
WIDTH = 256
BASE = 64
GROUP = 16
CHUNK = 8
VMEM = pl.BlockSpec(memory_space=pltpu.VMEM)
HBM = pl.BlockSpec(memory_space=pltpu.HBM)
SMEM = pl.BlockSpec(memory_space=pltpu.SMEM)


def dot(a, b, ca=1, cb=0):
    return lax.dot_general(
        a, b, (((ca,), (cb,)), ((), ())),
        precision=lax.Precision.HIGHEST, preferred_element_type=F32,
    )


def split(a):
    high = a.astype(jnp.bfloat16)
    return high, (a - high.astype(F32)).astype(jnp.bfloat16)


def dot_split(a, b):
    def part(x, y):
        return lax.dot_general(x, y, (((1,), (0,)), ((), ())), preferred_element_type=F32)

    (ah, al), (bh, bl) = split(a), b
    return part(ah, bh) + (part(ah, bl) + part(al, bh))


def targets_of(maps_ref, child, row, rows):
    cycles = maps_ref.shape[1] // rows
    targets = [maps_ref[child, rows * i + row] // rows for i in range(cycles)]
    first = jnp.int32(0)
    found = jnp.int32(0)
    for i in range(cycles):
        hit = targets[i] == 0
        first = jnp.where(hit, i, first)
        found = jnp.where(hit, 1, found)
    return targets, first, found


def slot_block(slot, first):
    if slot == 0:
        return first
    return jnp.where(first >= slot, slot - 1, slot)


def pick(values, at):
    out = values[0]
    for i in range(1, len(values)):
        out = jnp.where(at == i, values[i], out)
    return out


def child_of(parents_ref, front, which):
    found = jnp.int32(0)
    for d in range(parents_ref.shape[0] // 2):
        found = jnp.where(parents_ref[2 * d + which] == front, 2 * d + which, found)
    return found


def spread_kernel(children_ref, out_ref, hold_ref, sem):
    cycles = children_ref.shape[1]
    blocks = [(c, i) for c in range(2) for i in range(cycles)]
    copies = [
        pltpu.make_async_copy(children_ref.at[c, i], hold_ref.at[c, i], sem.at[c, i])
        for c, i in blocks
    ]
    for copy in copies:
        copy.start()
    for n, (c, i) in enumerate(blocks):
        copies[n].wait()
        for half in range(2):
            tiles = hold_ref[c, i, :, half * 128:(half + 1) * 128]
            out_ref[:, half, n * 8:(n + 1) * 8, :] = tiles.reshape(BLOCK // 8, 8, 128)


def plan_kernel(maps_ref, out_ref, *, rows):
    row = lax.axis_index("row")
    for c in range(maps_ref.shape[0]):
        out_ref[c] = targets_of(maps_ref, c, row, rows)[1]


def route_kernel(parents_ref, plan_ref, in_ref, first_ref, rest_ref):
    fronts, depth = in_ref.shape[0], in_ref.shape[1]
    cycles = depth // 16
    for d in range(fronts):
        for c in range(2):
            to = parents_ref[2 * d + c]
            first = plan_ref[2 * d + c]
            for s in range(cycles):
                at = pl.multiple_of((c * cycles + slot_block(s, first)) * 8, 8)
                tile = in_ref[d, pl.ds(at, 8), :]
                if s == 0:
                    first_ref[to, c * 8:(c + 1) * 8, :] = tile
                else:
                    put = (c * (cycles - 1) + s - 1) * 8
                    rest_ref[to, put:put + 8, :] = tile


def tile_block(ref, at):
    return jnp.concatenate(
        [ref[:, half, at:at + 8, :].reshape(BLOCK, 128) for half in range(2)], axis=1
    )


def top_kernel(parents_ref, maps_ref, panel_ref, pieces_ref, out_ref, first_ref, *, rows):
    front, row = lax.axis_index("front"), lax.axis_index("row")
    total = panel_ref[...]
    for c in range(2):
        first_ref[c] = tile_block(pieces_ref, c * 8)
        child = child_of(parents_ref, front, c)
        total += first_ref[c] * targets_of(maps_ref, child, row, rows)[2].astype(F32)
    out_ref[...] = total


def invert_base(a):
    n = a.shape[0]
    r = lax.broadcasted_iota(jnp.int32, (n, n), 0)
    l = lax.broadcasted_iota(jnp.int32, (n, n), 1)
    both = jnp.concatenate([a, jnp.where(r == l, 1.0, 0.0).astype(F32)], axis=1)
    done = []
    for g in range(0, n, GROUP):
        below = n - g
        sub = lax.broadcasted_iota(jnp.int32, (below, 2 * n), 0)
        columns = [
            jnp.broadcast_to(both[:, g + q:g + q + 1], (below, 2 * n)) for q in range(GROUP)
        ]
        diag = jnp.ones((GROUP, 2 * n), F32)
        for q in range(GROUP):
            column = columns[q]
            pivot = column[q:q + 1, :]
            diag = jnp.where(sub[:GROUP] == q, pivot, diag)
            f = jnp.where(sub > q, column, 0.0) * (1.0 / pivot)
            for k in range(q + 1, GROUP):
                columns[k] = columns[k] - f * columns[k][q:q + 1, :]
            both = both - f * both[q:q + 1, :]
        done.append(both[:GROUP] * lax.rsqrt(diag))
        both = both[GROUP:]
    return jnp.concatenate(done, axis=0)[:, n:]


def invert_factor(a):
    n = a.shape[0]
    if n == BASE:
        return invert_base(a)
    h = n // 2
    w1 = invert_factor(a[:h, :h])
    l21 = dot(a[h:, :h], w1, 1, 1)
    w2 = invert_factor(a[h:, h:] - dot(l21, l21, 1, 1))
    w21 = -dot(w2, dot(l21, w1))
    return jnp.concatenate(
        [
            jnp.concatenate([w1, jnp.zeros((h, h), F32)], axis=1),
            jnp.concatenate([w21, w2], axis=1),
        ],
        axis=0,
    )


def factor_kernel(pivots_ref, own_ref, r1_ref, r2_ref, r3_ref, first_ref, solve_ref, send_ref, all_ref):
    row = lax.axis_index("row")
    for s, ref in enumerate((own_ref, r1_ref, r2_ref, r3_ref)):
        at = pl.multiple_of(lax.rem(row + 4 - s, 4) * BLOCK, BLOCK)
        all_ref[pl.ds(at, BLOCK), :] = ref[...]
    pivots = pivots_ref[0]
    r = lax.broadcasted_iota(jnp.int32, (WIDTH, WIDTH), 0)
    l = lax.broadcasted_iota(jnp.int32, (WIDTH, WIDTH), 1)
    both = (r < pivots) & (l < pivots)
    diag = all_ref[0:WIDTH, :]
    low = jnp.where(r >= l, diag, 0.0)
    strict = jnp.where(r > l, diag, 0.0)
    mirrored = low + strict.T
    masked = jnp.where(both, mirrored, jnp.where(r == l, 1.0, 0.0))
    inverse = jnp.where(both, invert_factor(masked), 0.0)
    solved = dot(all_ref[...], inverse, 1, 1)
    top = jnp.where(r >= l, solved[:WIDTH], 0.0)
    solve_t = inverse - jnp.where(r < pivots, 0.0, dot(top, inverse))
    update_t = dot(solved[WIDTH:], inverse)
    solve_ref[...] = solve_t.T
    send_ref[0:WIDTH, :] = update_t.T
    send_ref[WIDTH:WIDTH + BLOCK, :] = own_ref[...]
    for c in range(2):
        at = WIDTH + (c + 1) * BLOCK
        send_ref[at:at + BLOCK, :] = first_ref[c]


def finish_kernel(parents_ref, maps_ref, orders_ref, pivots_ref, top_ref, solve_ref, sent_ref,
                  first_ref, rest_ref, lrest_ref, panel_ref, left_ref, out_ref,
                  hold_ref, x_ref, sem_hold, sem_x, sem_out, *, rows):
    front, row, col = lax.axis_index("front"), lax.axis_index("row"), lax.axis_index("col")
    cycles = panel_ref.shape[0]
    child_cycles = maps_ref.shape[1] // rows
    orders, pivots = orders_ref[0], pivots_ref[0]
    chunks = [pl.ds(k, CHUNK) for k in range(0, cycles, CHUNK)]
    hold = [
        pltpu.make_async_copy(panel_ref.at[at], hold_ref.at[at], sem_hold.at[k])
        for k, at in enumerate(chunks)
    ]
    store = [
        pltpu.make_async_copy(hold_ref.at[at], out_ref.at[at], sem_out.at[k])
        for k, at in enumerate(chunks)
    ]
    for k, at in enumerate(chunks):
        hold[k].start()

        @pl.when(col == 0)
        def _():
            pltpu.make_async_copy(panel_ref.at[at], x_ref.at[at], sem_x.at[k]).start()

        @pl.when(col != 0)
        def _():
            pltpu.make_async_copy(left_ref.at[at], x_ref.at[at], sem_x.at[k]).start()

    places = []
    for c in range(2):
        targets, first, _ = targets_of(maps_ref, child_of(parents_ref, front, c), row, rows)
        for s in range(child_cycles):
            places.append((pick(targets, slot_block(s, first)), c, s))

    left_first = [sent_ref.at[pl.ds(WIDTH + (c + 1) * BLOCK, BLOCK)] for c in range(2)]

    def child_block(first, rest, c, s):
        if s == 0:
            return first[c][...]
        return tile_block(rest, (c * (child_cycles - 1) + s - 1) * 8)

    lane = lax.broadcasted_iota(jnp.int32, (1, WIDTH), 1)
    scale = jnp.where((col != 0) | (lane >= pivots), 1.0, 0.0)
    right = split(jnp.where(col == 0, solve_ref[...], -sent_ref[0:WIDTH, :]))
    for k, at in enumerate(chunks):
        hold[k].wait()
        pltpu.make_async_copy(panel_ref.at[at], x_ref.at[at], sem_x.at[k]).wait()
        if k == 0:
            hold_ref[0] = top_ref[...]
            x_ref[0] = jnp.where(col == 0, top_ref[...], sent_ref[WIDTH:WIDTH + BLOCK, :])
        for place, c, s in places:
            @pl.when((place != 0) & (place // CHUNK == k))
            def _():
                hold_ref[place] += child_block(first_ref, rest_ref, c, s)

                @pl.when(col == 0)
                def _():
                    x_ref[place] += child_block(first_ref, rest_ref, c, s)

                @pl.when(col != 0)
                def _():
                    x_ref[place] += child_block(left_first, lrest_ref, c, s)

        y = dot_split(x_ref[at].reshape(CHUNK * BLOCK, WIDTH), right)
        for i in range(CHUNK):
            cycle = k * CHUNK + i
            start = (cycle * rows + row) * BLOCK
            z = hold_ref[cycle] * scale + y[i * BLOCK:(i + 1) * BLOCK]
            keep = start < orders
            if cycle == 0:
                g = row * BLOCK + lax.broadcasted_iota(jnp.int32, (BLOCK, WIDTH), 0)
                j = col * WIDTH + lax.broadcasted_iota(jnp.int32, (BLOCK, WIDTH), 1)
                keep = keep & (g >= j)
            hold_ref[cycle] = jnp.where(keep, z, 0.0)
        store[k].start()
    for copy in store:
        copy.wait()


def on_device(panel, children, parents, row_maps, orders, pivots):
    rows = lax.axis_size("row")
    fronts = lax.axis_size("front")
    cycles = panel.shape[1]
    child_cycles = children.shape[1]
    panel = panel[0]
    depth = 2 * (child_cycles - 1) * 8
    pieces = (BLOCK // 8, 2)
    params = pltpu.CompilerParams(vmem_limit_bytes=24 * 2**20)
    shape = lambda *dims: jax.ShapeDtypeStruct(dims, F32)
    to_right = [(0, 1)]

    def exchange(value):
        return lax.all_to_all(value.reshape(fronts, -1, 128), "front", 0, 0, tiled=True)

    left = lax.ppermute(panel, "col", to_right)
    spread = pl.pallas_call(
        spread_kernel, out_shape=shape(*pieces, depth + 16, 128),
        in_specs=[HBM], out_specs=VMEM,
        scratch_shapes=[
            pltpu.VMEM(children.shape, F32), pltpu.SemaphoreType.DMA((2, child_cycles)),
        ],
        compiler_params=pltpu.CompilerParams(vmem_limit_bytes=62 * 2**20), name="spread",
    )(children)
    spread = exchange(spread)
    plan = pl.pallas_call(
        lambda *refs: plan_kernel(*refs, rows=rows),
        out_shape=jax.ShapeDtypeStruct(parents.shape, jnp.int32),
        in_specs=[SMEM], out_specs=SMEM, name="plan",
    )(row_maps)
    first, rest = pl.pallas_call(
        route_kernel,
        out_shape=(shape(fronts, 16, 128), shape(fronts, depth, 128)),
        in_specs=[SMEM, SMEM, VMEM], out_specs=(VMEM, VMEM), compiler_params=params, name="route",
    )(parents, plan, spread)
    first, panel = lax.optimization_barrier((first, panel))
    first = exchange(first)
    panel_top = panel[0]
    top, first = pl.pallas_call(
        lambda *refs: top_kernel(*refs, rows=rows),
        out_shape=(shape(BLOCK, WIDTH), shape(2, BLOCK, WIDTH)),
        in_specs=[SMEM, SMEM, VMEM, VMEM], out_specs=(VMEM, VMEM),
        compiler_params=params, name="top",
    )(parents, row_maps, panel_top, first.reshape(*pieces, 16, 128))
    rest, top = lax.optimization_barrier((rest, top))
    rest = exchange(rest).reshape(*pieces, depth, 128)
    others = [
        lax.ppermute(top, "row", [(i, (i + s) % rows) for i in range(rows)]) for s in (1, 2, 3)
    ]
    solve, send = pl.pallas_call(
        factor_kernel,
        out_shape=(shape(WIDTH, WIDTH), shape(WIDTH + 3 * BLOCK, WIDTH)),
        in_specs=[SMEM] + [VMEM] * 5, out_specs=(VMEM, VMEM),
        scratch_shapes=[pltpu.VMEM((4 * BLOCK, WIDTH), F32)],
        compiler_params=params, name="factor",
        cost_estimate=pl.CostEstimate(flops=2 * 10**9, bytes_accessed=2**21, transcendentals=0),
    )(pivots, top, *others, first)
    sent = lax.ppermute(send, "col", to_right)

    rest, solve = lax.optimization_barrier((rest, solve))
    left_rest = lax.ppermute(rest, "col", to_right)
    steps = cycles // CHUNK
    out = pl.pallas_call(
        lambda *refs: finish_kernel(*refs, rows=rows),
        out_shape=shape(*panel.shape),
        in_specs=[SMEM] * 4 + [VMEM] * 6 + [HBM] * 2, out_specs=HBM,
        scratch_shapes=[pltpu.VMEM(panel.shape, F32)] * 2 + [pltpu.SemaphoreType.DMA((steps,))] * 3,
        compiler_params=pltpu.CompilerParams(vmem_limit_bytes=24 * 2**20), name="finish",
        cost_estimate=pl.CostEstimate(flops=10**9, bytes_accessed=12 * 2**20, transcendentals=0),
    )(
        parents, row_maps, orders, pivots, top, solve, sent,
        first, rest, left_rest, panel, left,
    )
    return out[None]


def solution(mesh):
    in_specs = (
        P("front", None, "row", "col"),
        P("front", None, "row", "col"),
        P(),
        P(),
        P("front"),
        P("front"),
    )
    out_specs = P("front", None, "row", "col")
    return jax.shard_map(
        on_device, mesh=mesh, in_specs=in_specs, out_specs=out_specs, check_vma=False
    )
```

```python
import jax
import jax.numpy as jnp
from jax import lax
from jax.experimental import pallas as pl
from jax.experimental.pallas import tpu as pltpu
from jax.sharding import PartitionSpec as P

F32 = jnp.float32
BLOCK = 128
WIDTH = 256
BASE = 64
GROUP = 16
CHUNK = 8
VMEM = pl.BlockSpec(memory_space=pltpu.VMEM)
HBM = pl.BlockSpec(memory_space=pltpu.HBM)
SMEM = pl.BlockSpec(memory_space=pltpu.SMEM)


def dot(a, b, ca=1, cb=0):
    return lax.dot_general(
        a, b, (((ca,), (cb,)), ((), ())),
        precision=lax.Precision.HIGHEST, preferred_element_type=F32,
    )


def split(a):
    high = a.astype(jnp.bfloat16)
    return high, (a - high.astype(F32)).astype(jnp.bfloat16)


def dot_split(a, b):
    def part(x, y):
        return lax.dot_general(x, y, (((1,), (0,)), ((), ())), preferred_element_type=F32)

    (ah, al), (bh, bl) = split(a), b
    return part(ah, bh) + (part(ah, bl) + part(al, bh))


def targets_of(maps_ref, child, row, rows):
    cycles = maps_ref.shape[1] // rows
    targets = [maps_ref[child, rows * i + row] // rows for i in range(cycles)]
    first = jnp.int32(0)
    found = jnp.int32(0)
    for i in range(cycles):
        hit = targets[i] == 0
        first = jnp.where(hit, i, first)
        found = jnp.where(hit, 1, found)
    return targets, first, found


def slot_block(slot, first):
    if slot == 0:
        return first
    return jnp.where(first >= slot, slot - 1, slot)


def pick(values, at):
    out = values[0]
    for i in range(1, len(values)):
        out = jnp.where(at == i, values[i], out)
    return out


def child_of(parents_ref, front, which):
    found = jnp.int32(0)
    for d in range(parents_ref.shape[0] // 2):
        found = jnp.where(parents_ref[2 * d + which] == front, 2 * d + which, found)
    return found


def spread_kernel(children_ref, panel_ref, out_ref, top_ref, hold_ref, sem, sem_top):
    cycles = children_ref.shape[1]
    blocks = [(c, i) for c in range(2) for i in range(cycles)]
    copies = [
        pltpu.make_async_copy(children_ref.at[c, i], hold_ref.at[c, i], sem.at[c, i])
        for c, i in blocks
    ]
    for copy in copies:
        copy.start()
    top = pltpu.make_async_copy(panel_ref.at[0], top_ref, sem_top)
    top.start()
    for n, (c, i) in enumerate(blocks):
        copies[n].wait()
        for half in range(2):
            tiles = hold_ref[c, i, :, half * 128:(half + 1) * 128]
            out_ref[:, half, n * 8:(n + 1) * 8, :] = tiles.reshape(BLOCK // 8, 8, 128)
    top.wait()


def plan_kernel(maps_ref, out_ref, *, rows):
    row = lax.axis_index("row")
    for c in range(maps_ref.shape[0]):
        out_ref[c] = targets_of(maps_ref, c, row, rows)[1]


def route_kernel(parents_ref, plan_ref, in_ref, first_ref, rest_ref):
    fronts, depth = in_ref.shape[0], in_ref.shape[1]
    cycles = depth // 16
    for d in range(fronts):
        for c in range(2):
            to = parents_ref[2 * d + c]
            first = plan_ref[2 * d + c]
            for s in range(cycles):
                at = pl.multiple_of((c * cycles + slot_block(s, first)) * 8, 8)
                tile = in_ref[d, pl.ds(at, 8), :]
                if s == 0:
                    first_ref[to, c * 8:(c + 1) * 8, :] = tile
                else:
                    put = (c * (cycles - 1) + s - 1) * 8
                    rest_ref[to, put:put + 8, :] = tile


def tile_block(ref, at):
    return jnp.concatenate(
        [ref[:, half, at:at + 8, :].reshape(BLOCK, 128) for half in range(2)], axis=1
    )


def top_kernel(parents_ref, maps_ref, panel_ref, pieces_ref, out_ref, first_ref, *, rows):
    front, row = lax.axis_index("front"), lax.axis_index("row")
    total = panel_ref[...]
    for c in range(2):
        first_ref[c] = tile_block(pieces_ref, c * 8)
        child = child_of(parents_ref, front, c)
        total += first_ref[c] * targets_of(maps_ref, child, row, rows)[2].astype(F32)
    out_ref[...] = total


def invert_base(a):
    n = a.shape[0]
    r = lax.broadcasted_iota(jnp.int32, (n, n), 0)
    l = lax.broadcasted_iota(jnp.int32, (n, n), 1)
    both = jnp.concatenate([a, jnp.where(r == l, 1.0, 0.0).astype(F32)], axis=1)
    done = []
    for g in range(0, n, GROUP):
        below = n - g
        sub = lax.broadcasted_iota(jnp.int32, (below, 2 * n), 0)
        columns = [
            jnp.broadcast_to(both[:, g + q:g + q + 1], (below, 2 * n)) for q in range(GROUP)
        ]
        diag = jnp.ones((GROUP, 2 * n), F32)
        for q in range(GROUP):
            column = columns[q]
            pivot = column[q:q + 1, :]
            diag = jnp.where(sub[:GROUP] == q, pivot, diag)
            f = jnp.where(sub > q, column, 0.0) * (1.0 / pivot)
            for k in range(q + 1, GROUP):
                columns[k] = columns[k] - f * columns[k][q:q + 1, :]
            both = both - f * both[q:q + 1, :]
        done.append(both[:GROUP] * lax.rsqrt(diag))
        both = both[GROUP:]
    return jnp.concatenate(done, axis=0)[:, n:]


def invert_factor(a):
    n = a.shape[0]
    if n == BASE:
        return invert_base(a)
    h = n // 2
    w1 = invert_factor(a[:h, :h])
    l21 = dot(a[h:, :h], w1, 1, 1)
    w2 = invert_factor(a[h:, h:] - dot(l21, l21, 1, 1))
    w21 = -dot(w2, dot(l21, w1))
    return jnp.concatenate(
        [
            jnp.concatenate([w1, jnp.zeros((h, h), F32)], axis=1),
            jnp.concatenate([w21, w2], axis=1),
        ],
        axis=0,
    )


def factor_kernel(pivots_ref, own_ref, r1_ref, r2_ref, r3_ref, first_ref, solve_ref, send_ref, all_ref):
    row = lax.axis_index("row")
    for s, ref in enumerate((own_ref, r1_ref, r2_ref, r3_ref)):
        at = pl.multiple_of(lax.rem(row + 4 - s, 4) * BLOCK, BLOCK)
        all_ref[pl.ds(at, BLOCK), :] = ref[...]
    pivots = pivots_ref[0]
    r = lax.broadcasted_iota(jnp.int32, (WIDTH, WIDTH), 0)
    l = lax.broadcasted_iota(jnp.int32, (WIDTH, WIDTH), 1)
    both = (r < pivots) & (l < pivots)
    diag = all_ref[0:WIDTH, :]
    low = jnp.where(r >= l, diag, 0.0)
    strict = jnp.where(r > l, diag, 0.0)
    mirrored = low + strict.T
    masked = jnp.where(both, mirrored, jnp.where(r == l, 1.0, 0.0))
    inverse = jnp.where(both, invert_factor(masked), 0.0)
    solved = dot(all_ref[...], inverse, 1, 1)
    top = jnp.where(r >= l, solved[:WIDTH], 0.0)
    solve_t = inverse - jnp.where(r < pivots, 0.0, dot(top, inverse))
    update_t = dot(solved[WIDTH:], inverse)
    solve_ref[...] = solve_t.T
    send_ref[0:WIDTH, :] = update_t.T
    send_ref[WIDTH:WIDTH + BLOCK, :] = own_ref[...]
    for c in range(2):
        at = WIDTH + (c + 1) * BLOCK
        send_ref[at:at + BLOCK, :] = first_ref[c]


def finish_kernel(parents_ref, maps_ref, orders_ref, pivots_ref, top_ref, solve_ref, sent_ref,
                  first_ref, rest_ref, lrest_ref, panel_ref, left_ref, out_ref,
                  hold_ref, x_ref, sem_hold, sem_x, sem_out, *, rows):
    front, row, col = lax.axis_index("front"), lax.axis_index("row"), lax.axis_index("col")
    cycles = panel_ref.shape[0]
    child_cycles = maps_ref.shape[1] // rows
    orders, pivots = orders_ref[0], pivots_ref[0]
    chunks = [pl.ds(k, CHUNK) for k in range(0, cycles, CHUNK)]
    hold = [
        pltpu.make_async_copy(panel_ref.at[at], hold_ref.at[at], sem_hold.at[k])
        for k, at in enumerate(chunks)
    ]
    store = [
        pltpu.make_async_copy(hold_ref.at[at], out_ref.at[at], sem_out.at[k])
        for k, at in enumerate(chunks)
    ]
    for k, at in enumerate(chunks):
        hold[k].start()

        @pl.when(col == 0)
        def _():
            pltpu.make_async_copy(panel_ref.at[at], x_ref.at[at], sem_x.at[k]).start()

        @pl.when(col != 0)
        def _():
            pltpu.make_async_copy(left_ref.at[at], x_ref.at[at], sem_x.at[k]).start()

    places = []
    for c in range(2):
        targets, first, _ = targets_of(maps_ref, child_of(parents_ref, front, c), row, rows)
        for s in range(child_cycles):
            places.append((pick(targets, slot_block(s, first)), c, s))

    left_first = [sent_ref.at[pl.ds(WIDTH + (c + 1) * BLOCK, BLOCK)] for c in range(2)]

    def child_block(first, rest, c, s):
        if s == 0:
            return first[c][...]
        return tile_block(rest, (c * (child_cycles - 1) + s - 1) * 8)

    lane = lax.broadcasted_iota(jnp.int32, (1, WIDTH), 1)
    scale = jnp.where((col != 0) | (lane >= pivots), 1.0, 0.0)
    right = split(jnp.where(col == 0, solve_ref[...], -sent_ref[0:WIDTH, :]))
    for k, at in enumerate(chunks):
        hold[k].wait()
        pltpu.make_async_copy(panel_ref.at[at], x_ref.at[at], sem_x.at[k]).wait()
        if k == 0:
            hold_ref[0] = top_ref[...]
            x_ref[0] = jnp.where(col == 0, top_ref[...], sent_ref[WIDTH:WIDTH + BLOCK, :])
        for place, c, s in places:
            @pl.when((place != 0) & (place // CHUNK == k))
            def _():
                hold_ref[place] += child_block(first_ref, rest_ref, c, s)

                @pl.when(col == 0)
                def _():
                    x_ref[place] += child_block(first_ref, rest_ref, c, s)

                @pl.when(col != 0)
                def _():
                    x_ref[place] += child_block(left_first, lrest_ref, c, s)

        y = dot_split(x_ref[at].reshape(CHUNK * BLOCK, WIDTH), right)
        for i in range(CHUNK):
            cycle = k * CHUNK + i
            start = (cycle * rows + row) * BLOCK
            z = hold_ref[cycle] * scale + y[i * BLOCK:(i + 1) * BLOCK]
            keep = start < orders
            if cycle == 0:
                g = row * BLOCK + lax.broadcasted_iota(jnp.int32, (BLOCK, WIDTH), 0)
                j = col * WIDTH + lax.broadcasted_iota(jnp.int32, (BLOCK, WIDTH), 1)
                keep = keep & (g >= j)
            hold_ref[cycle] = jnp.where(keep, z, 0.0)
        store[k].start()
    for copy in store:
        copy.wait()


def on_device(panel, children, parents, row_maps, orders, pivots):
    rows = lax.axis_size("row")
    fronts = lax.axis_size("front")
    cycles = panel.shape[1]
    child_cycles = children.shape[1]
    panel = panel[0]
    depth = 2 * (child_cycles - 1) * 8
    pieces = (BLOCK // 8, 2)
    params = pltpu.CompilerParams(vmem_limit_bytes=24 * 2**20)
    shape = lambda *dims: jax.ShapeDtypeStruct(dims, F32)
    to_right = [(0, 1)]

    def exchange(value):
        return lax.all_to_all(value.reshape(fronts, -1, 128), "front", 0, 0, tiled=True)

    left = lax.ppermute(panel, "col", to_right)
    spread, panel_top = pl.pallas_call(
        spread_kernel, out_shape=(shape(*pieces, depth + 16, 128), shape(BLOCK, WIDTH)),
        in_specs=[HBM, HBM], out_specs=(VMEM, VMEM),
        scratch_shapes=[
            pltpu.VMEM(children.shape, F32), pltpu.SemaphoreType.DMA((2, child_cycles)),
            pltpu.SemaphoreType.DMA,
        ],
        compiler_params=pltpu.CompilerParams(vmem_limit_bytes=62 * 2**20), name="spread",
    )(children, panel)
    spread = exchange(spread)
    plan = pl.pallas_call(
        lambda *refs: plan_kernel(*refs, rows=rows),
        out_shape=jax.ShapeDtypeStruct(parents.shape, jnp.int32),
        in_specs=[SMEM], out_specs=SMEM, name="plan",
    )(row_maps)
    first, rest = pl.pallas_call(
        route_kernel,
        out_shape=(shape(fronts, 16, 128), shape(fronts, depth, 128)),
        in_specs=[SMEM, SMEM, VMEM], out_specs=(VMEM, VMEM), compiler_params=params, name="route",
    )(parents, plan, spread)
    first = exchange(first)
    top, first = pl.pallas_call(
        lambda *refs: top_kernel(*refs, rows=rows),
        out_shape=(shape(BLOCK, WIDTH), shape(2, BLOCK, WIDTH)),
        in_specs=[SMEM, SMEM, VMEM, VMEM], out_specs=(VMEM, VMEM),
        compiler_params=params, name="top",
    )(parents, row_maps, panel_top, first.reshape(*pieces, 16, 128))
    rest, top = lax.optimization_barrier((rest, top))
    rest = exchange(rest).reshape(*pieces, depth, 128)
    others = [
        lax.ppermute(top, "row", [(i, (i + s) % rows) for i in range(rows)]) for s in (1, 2, 3)
    ]
    solve, send = pl.pallas_call(
        factor_kernel,
        out_shape=(shape(WIDTH, WIDTH), shape(WIDTH + 3 * BLOCK, WIDTH)),
        in_specs=[SMEM] + [VMEM] * 5, out_specs=(VMEM, VMEM),
        scratch_shapes=[pltpu.VMEM((4 * BLOCK, WIDTH), F32)],
        compiler_params=params, name="factor",
        cost_estimate=pl.CostEstimate(flops=2 * 10**9, bytes_accessed=2**21, transcendentals=0),
    )(pivots, top, *others, first)
    sent = lax.ppermute(send, "col", to_right)

    rest, solve = lax.optimization_barrier((rest, solve))
    left_rest = lax.ppermute(rest, "col", to_right)
    steps = cycles // CHUNK
    out = pl.pallas_call(
        lambda *refs: finish_kernel(*refs, rows=rows),
        out_shape=shape(*panel.shape),
        in_specs=[SMEM] * 4 + [VMEM] * 6 + [HBM] * 2, out_specs=HBM,
        scratch_shapes=[pltpu.VMEM(panel.shape, F32)] * 2 + [pltpu.SemaphoreType.DMA((steps,))] * 3,
        compiler_params=pltpu.CompilerParams(vmem_limit_bytes=24 * 2**20), name="finish",
        cost_estimate=pl.CostEstimate(flops=10**9, bytes_accessed=12 * 2**20, transcendentals=0),
    )(
        parents, row_maps, orders, pivots, top, solve, sent,
        first, rest, left_rest, panel, left,
    )
    return out[None]


def solution(mesh):
    in_specs = (
        P("front", None, "row", "col"),
        P("front", None, "row", "col"),
        P(),
        P(),
        P("front"),
        P("front"),
    )
    out_specs = P("front", None, "row", "col")
    return jax.shard_map(
        on_device, mesh=mesh, in_specs=in_specs, out_specs=out_specs, check_vma=False
    )
```
